32 devices in a mesh: groups: 2 (over y), graph: 4 (over z), tm: 2 (over x), rep: 2 (over core).
Axes of the slice: x: 2, y: 2, z: 4, core: 2. Of those that a mesh axis runs over, the one named last changes fastest.
Arguments:
- probes: bfloat16 [16, 128, 4096], P(('groups', 'rep'), 'tm', 'graph'), parts along dimension 0, may hold values from -6 to 6
- lap_blocks: bfloat16 [64, 4, 128, 128], P(('groups', 'graph')), parts along dimension 0, may hold values from -0.1875 to 0.1875
- col_index: int32 [64, 4], P(('groups', 'graph')), parts along dimension 0, may hold values from 0 to 15, as said below
- series_weights: float32 [4], replicated, may hold values from 0.3 to 1
- hour_band: float32 [33, 128], P(None, 'tm'), may hold values from -1 to 1
Outputs:
- kernel_product: bfloat16 [16, 128, 4096], P(('groups', 'rep'), 'tm', 'graph'), parts along dimension 0
The draws below stay inside these ranges and needn't reach their ends.
There are 2 independent parts, one for each index of `groups`. The reference program is written for one: setup_inputs(seed, part) draws one part's arguments, and reference() takes and returns one part's arrays. A program takes and returns all parts, laid end to end along the dimension named above; an argument that names none is the same for every part. Nothing has to cross between parts.
Inputs may be any that keep to these rules, and one draw needn't show every extreme that they name: `col_index`: let r be a block row's number within its part (global row mod 8). Entry 0 is r + 4. Numbers 4 to 11 are the part's own blocks; 0 to 3 are the previous part's last 4 blocks, named only by rows r < 4; 12 to 15 are the next part's first 4 blocks, named only by rows r >= 4.
All inputs are finite; a program needn't handle non-finite values.
Results may differ from the reference program's by a relative error of at most 0.0059.
Values may be sent and summed in bfloat16 or wider, within the bound.
A program may use at most 64 MiB of HBM per device.

```python
import jax
import jax.numpy as jnp
from jax import lax

BLK = 128
NNZ = 4
BND = 4
BAND = 16
BANDW = 33
NB = 8
NBLK = 32
NODES = 4096
HOURS = 128
PROBES = 8


def draw_col_index(key, part):
    key = jax.random.fold_in(key, 7)
    row_pos = jnp.arange(NBLK, dtype=jnp.int32) % NB
    low_end = jnp.where(row_pos < BND, 0, BND).astype(jnp.int32)
    high_end = jnp.where(row_pos >= NB - BND, NB + 2 * BND, NB + BND).astype(jnp.int32)
    picked = jax.random.randint(key, (NBLK, NNZ), low_end[:, None], high_end[:, None], dtype=jnp.int32)
    diagonal_col = row_pos + BND
    second_col = jnp.where(row_pos < BND, row_pos, jnp.where(row_pos >= NB - BND, row_pos + 2 * BND, picked[:, 1]))
    picked = picked.at[:, 0].set(diagonal_col).at[:, 1].set(second_col)
    return picked.astype(jnp.int32)


def steps_of(stream_key, shape, pieces, low, largest):
    loudness, own = 1.0, jax.random.fold_in(stream_key, 6)
    for position, parts in pieces:
        draws = jnp.exp(jax.random.uniform(jax.random.fold_in(own, position), (parts,), jnp.float32, low / len(pieces), largest / len(pieces)))
        loudness = loudness * jnp.repeat(draws, shape[position] // parts).reshape([-1 if axis == position else 1 for axis in range(len(shape))])
    return loudness


def centred(own_key, shape, deviation, bound, pieces=(), kind=jnp.bfloat16):
    gain = steps_of(own_key, shape, pieces, -0.22, 0.18) if pieces else 1.0
    drawn = jax.random.normal(own_key, shape, jnp.float32) * deviation * gain
    return jnp.minimum(jnp.maximum(drawn, -bound), bound).astype(kind)


def setup_inputs(seed: int = 0, part: int = 0) -> dict:
    key_of = jax.random.split(jax.random.key(seed), 6)
    part_keys = jax.random.split(jax.random.fold_in(key_of[5], part), 6)
    return {
        "probes": centred(part_keys[0], (PROBES, HOURS, NODES), 1.0, 6.0, ((0, 2), (1, 2), (2, 4))),
        "lap_blocks": centred(part_keys[1], (NBLK, NNZ, BLK, BLK), (2 * NNZ * BLK) ** -0.5, 0.1875, ((0, 4),)),
        "col_index": draw_col_index(jax.random.fold_in(jax.random.fold_in(key_of[5], part), 71), part),
        "series_weights": jnp.clip(jax.random.uniform(key_of[3], (4,), jnp.float32, 0.3, 1.0), 0.3, 1.0),
        "hour_band": centred(key_of[4], (BANDW, HOURS), BANDW ** -0.5, 1.0, ((1, 2),), jnp.float32),
    }


def graph_apply(field, lap_blocks, col_index):
    probe_count, hour_count, node_count = field.shape
    row_count = probe_count * hour_count
    padded = jnp.pad(field, ((0, 0), (0, 0), (BND * BLK, BND * BLK))).reshape(row_count, NBLK + 2 * BND, BLK)
    base_block = (jnp.arange(NBLK, dtype=jnp.int32) // NB) * NB
    where_cols = (base_block[:, None] + col_index).astype(jnp.int32)

    def one_row(index):
        picked = jnp.take(padded, where_cols[index], axis=1).astype(jnp.float32)
        return jnp.einsum("rkj,kij->ri", picked, lap_blocks[index].astype(jnp.float32))

    stacked = lax.map(one_row, jnp.arange(NBLK, dtype=jnp.int32))
    return stacked.transpose(1, 0, 2).reshape(probe_count, hour_count, node_count)


def reference(probes, lap_blocks, col_index, series_weights, hour_band):
    term_one = graph_apply(probes, lap_blocks, col_index)
    rounded_one = term_one.astype(jnp.bfloat16)
    term_two = 2.0 * graph_apply(rounded_one, lap_blocks, col_index) - probes.astype(jnp.float32)
    rounded_two = term_two.astype(jnp.bfloat16)
    term_three = 2.0 * graph_apply(rounded_two, lap_blocks, col_index) - term_one
    mixed = (series_weights[0] * probes.astype(jnp.float32) + series_weights[1] * term_one
             + series_weights[2] * term_two + series_weights[3] * term_three).astype(jnp.bfloat16)
    padded = jnp.pad(mixed, ((0, 0), (BAND, BAND), (0, 0)))
    total = jnp.zeros(mixed.shape, jnp.float32)
    for offset in range(2 * BAND + 1):
        total = total + hour_band[offset][None, :, None] * padded[:, offset:offset + HOURS].astype(jnp.float32)
    return total.astype(jnp.bfloat16)
```

```python
import functools

import jax
import jax.numpy as jnp
from jax import lax
from jax.experimental import pallas as pl
from jax.experimental.pallas import tpu as pltpu
from jax.sharding import PartitionSpec as P

BLK = 128
NNZ = 4
BND = 4
BAND = 16
BANDW = 33
GROUP = 16
TERMS = 3


def kernel(
    graph_size,
    tm_size,
    probes,
    lap,
    col,
    weights,
    hour_band,
    out,
    *scratch,
):
    probe_count, hour_count, node_count = probes.shape
    row_blocks = node_count // BLK
    group_count = hour_count // GROUP
    rows = probe_count * GROUP
    extended = scratch[: TERMS * group_count]
    (
        staged,
        lap_held,
        lap_turned,
        one,
        two,
        mixed,
        factor,
        own_sem,
        lap_sem,
        send_sem,
        recv_sem,
        edge_send_sem,
        edge_recv_sem,
    ) = scratch[TERMS * group_count :]
    order = [0, group_count - 1] + list(range(1, group_count - 1))

    def ext(term, group):
        return extended[term * group_count + group]

    def hours_of(group):
        return pl.ds(group * GROUP, GROUP)

    place = lax.axis_index("graph")
    slab = lax.axis_index("tm")
    has_low, has_high = place > 0, place < graph_size - 1
    has_before, has_after = slab > 0, slab < tm_size - 1

    def own_copy(group):
        return pltpu.make_async_copy(
            probes.at[:, hours_of(group), :],
            staged.at[:, hours_of(group), :],
            own_sem.at[group],
        )

    lap_copy = pltpu.make_async_copy(lap, lap_held, lap_sem)
    lap_copy.start()
    for group in order:
        own_copy(group).start()

    def to_high(term, group):
        return pltpu.make_async_remote_copy(
            src_ref=ext(term, group).at[pl.ds(row_blocks, BND)],
            dst_ref=ext(term, group).at[pl.ds(0, BND)],
            send_sem=send_sem.at[term, group, 0],
            recv_sem=recv_sem.at[term, group, 0],
            device_id={"graph": place + 1},
            device_id_type=pl.DeviceIdType.MESH,
        )

    def to_low(term, group):
        return pltpu.make_async_remote_copy(
            src_ref=ext(term, group).at[pl.ds(BND, BND)],
            dst_ref=ext(term, group).at[pl.ds(BND + row_blocks, BND)],
            send_sem=send_sem.at[term, group, 1],
            recv_sem=recv_sem.at[term, group, 1],
            device_id={"graph": place - 1},
            device_id_type=pl.DeviceIdType.MESH,
        )

    def to_after():
        return pltpu.make_async_remote_copy(
            src_ref=mixed.at[:, pl.ds(hour_count, BAND), :],
            dst_ref=mixed.at[:, pl.ds(0, BAND), :],
            send_sem=edge_send_sem.at[0],
            recv_sem=edge_recv_sem.at[0],
            device_id={"tm": slab + 1},
            device_id_type=pl.DeviceIdType.MESH,
        )

    def to_before():
        return pltpu.make_async_remote_copy(
            src_ref=mixed.at[:, pl.ds(BAND, BAND), :],
            dst_ref=mixed.at[:, pl.ds(BAND + hour_count, BAND), :],
            send_sem=edge_send_sem.at[1],
            recv_sem=edge_recv_sem.at[1],
            device_id={"tm": slab - 1},
            device_id_type=pl.DeviceIdType.MESH,
        )

    barrier = pltpu.get_barrier_semaphore()
    neighbours = (
        (has_low, {"graph": place - 1}),
        (has_high, {"graph": place + 1}),
        (has_before, {"tm": slab - 1}),
        (has_after, {"tm": slab + 1}),
    )
    for there, device in neighbours:

        @pl.when(there)
        def _(device=device):
            pl.semaphore_signal(
                barrier, inc=1, device_id=device, device_id_type=pl.DeviceIdType.MESH
            )

    def take_own(group):
        own_copy(group).wait()
        for block in range(row_blocks):
            ext(0, group)[BND + block] = staged[
                :, hours_of(group), pl.ds(block * BLK, BLK)
            ]

    take_own(order[0])
    peers = sum(jnp.where(there, 1, 0) for there, _ in neighbours)
    pl.semaphore_wait(barrier, peers)

    for group in order:
        if group != order[0]:
            take_own(group)

        @pl.when(has_high)
        def _(group=group):
            to_high(0, group).start()

        @pl.when(has_low)
        def _(group=group):
            to_low(0, group).start()

    @pl.when(jnp.logical_not(has_low))
    def _():
        for ref in extended:
            ref[pl.ds(0, BND)] = jnp.zeros((BND, probe_count, GROUP, BLK), jnp.bfloat16)

    @pl.when(jnp.logical_not(has_high))
    def _():
        for ref in extended:
            ref[pl.ds(BND + row_blocks, BND)] = jnp.zeros(
                (BND, probe_count, GROUP, BLK), jnp.bfloat16
            )

    @pl.when(jnp.logical_not(has_before))
    def _():
        mixed[:, pl.ds(0, BAND), :] = jnp.zeros((probe_count, BAND, node_count), jnp.bfloat16)

    @pl.when(jnp.logical_not(has_after))
    def _():
        mixed[:, pl.ds(BAND + hour_count, BAND), :] = jnp.zeros(
            (probe_count, BAND, node_count), jnp.bfloat16
        )

    span = hour_count + 2 * BAND
    hour_in = lax.broadcasted_iota(jnp.int32, (span, hour_count), 0)
    hour_out = lax.broadcasted_iota(jnp.int32, (span, hour_count), 1)
    shift = hour_in - hour_out
    turned = jnp.zeros((span, hour_count), jnp.float32)
    for offset in range(BANDW):
        turned = jnp.where(shift == offset, hour_band[pl.ds(offset, 1), :], turned)
    turned = jnp.concatenate(
        [turned, jnp.zeros((span, 128 - hour_count), jnp.float32)], axis=1
    )
    turned = jnp.concatenate([turned, jnp.zeros((128 - span, 128), jnp.float32)], axis=0)
    whole = turned.T[:hour_count]
    high = whole.astype(jnp.bfloat16)
    low = (whole - high.astype(jnp.float32)).astype(jnp.bfloat16)
    factor[pl.ds(0, hour_count), :] = high
    factor[pl.ds(hour_count, hour_count), :] = low

    lap_copy.wait()

    def turn(row, carry):
        for entry in range(NNZ):
            lap_turned[row, pl.ds(entry * BLK, BLK), :] = lap_held[row, entry].T
        return carry

    lax.fori_loop(0, row_blocks, turn, 0)

    def lanes(block):
        return pl.ds(pl.multiple_of(block * BLK, BLK), BLK)

    def rows_of(term, group, first, count):
        source = ext(term, group)
        hours = hours_of(group)

        def body(row, carry):
            parts = [source[row + BND]]
            for entry in range(1, NNZ):
                parts.append(source[col[entry, row]])
            gathered = jnp.concatenate(
                [part.reshape(rows, BLK) for part in parts], axis=1
            )
            product = jnp.dot(
                gathered, lap_turned[row], preferred_element_type=jnp.float32
            ).reshape(probe_count, GROUP, BLK)
            here = lanes(row)
            if term == 0:
                one[:, hours, here] = product
                ext(1, group)[row + BND] = product.astype(jnp.bfloat16)
            elif term == 1:
                start = ext(0, group)[row + BND].astype(jnp.float32)
                value = 2.0 * product - start
                two[:, hours, here] = value
                ext(2, group)[row + BND] = value.astype(jnp.bfloat16)
            else:
                start = ext(0, group)[row + BND].astype(jnp.float32)
                first_term = one[:, hours, here]
                value = 2.0 * product - first_term
                mixed[:, pl.ds(BAND + group * GROUP, GROUP), here] = (
                    weights[0] * start
                    + weights[1] * first_term
                    + weights[2] * two[:, hours, here]
                    + weights[3] * value
                ).astype(jnp.bfloat16)
            return carry

        lax.fori_loop(first, first + count, body, 0, unroll=True)

    for term in range(TERMS):
        for group in order:

            @pl.when(has_low)
            def _(term=term, group=group):
                to_high(term, group).wait_recv()

            @pl.when(has_high)
            def _(term=term, group=group):
                to_low(term, group).wait_recv()

            rows_of(term, group, 0, BND)
            if term < TERMS - 1:

                @pl.when(has_low)
                def _(term=term, group=group):
                    to_low(term + 1, group).start()

            rows_of(term, group, BND, row_blocks - BND)
            if term < TERMS - 1:

                @pl.when(has_high)
                def _(term=term, group=group):
                    to_high(term + 1, group).start()

            elif group == 0:

                @pl.when(has_before)
                def _():
                    to_before().start()

            elif group == group_count - 1:

                @pl.when(has_after)
                def _():
                    to_after().start()

    @pl.when(has_before)
    def _():
        to_after().wait_recv()

    @pl.when(has_after)
    def _():
        to_before().wait_recv()

    width = 256

    def spread(index, carry):
        probe = index // (node_count // width)
        here = pl.ds(pl.multiple_of((index % (node_count // width)) * width, width), width)
        both = jnp.dot(
            factor[:, pl.ds(0, span)],
            mixed[probe, :, here],
            preferred_element_type=jnp.float32,
        )
        out[probe, :, here] = (both[:hour_count] + both[hour_count:]).astype(jnp.bfloat16)
        return carry

    lax.fori_loop(0, probe_count * (node_count // width), spread, 0, unroll=True)

    for term in range(TERMS):
        for group in order:

            @pl.when(has_high)
            def _(term=term, group=group):
                to_high(term, group).wait_send()

            @pl.when(has_low)
            def _(term=term, group=group):
                to_low(term, group).wait_send()

    @pl.when(has_after)
    def _():
        to_after().wait_send()

    @pl.when(has_before)
    def _():
        to_before().wait_send()


def shards(graph_size, tm_size, probes, lap_blocks, col_index, series_weights, hour_band):
    probe_count, hour_count, node_count = probes.shape
    row_blocks = node_count // BLK
    groups = hour_count // GROUP
    field = (probe_count, hour_count, node_count)
    vmem = pl.BlockSpec(memory_space=pltpu.VMEM)
    smem = pl.BlockSpec(memory_space=pltpu.SMEM)
    far = pl.BlockSpec(memory_space=pltpu.HBM)
    return pl.pallas_call(
        functools.partial(kernel, graph_size, tm_size),
        out_shape=jax.ShapeDtypeStruct(field, jnp.bfloat16),
        in_specs=[far, far, smem, smem, vmem],
        out_specs=vmem,
        scratch_shapes=[
            pltpu.VMEM((row_blocks + 2 * BND, probe_count, GROUP, BLK), jnp.bfloat16)
            for _ in range(TERMS * groups)
        ]
        + [
            pltpu.VMEM(field, jnp.bfloat16),
            pltpu.VMEM(lap_blocks.shape, jnp.bfloat16),
            pltpu.VMEM((row_blocks, NNZ * BLK, BLK), jnp.bfloat16),
            pltpu.VMEM(field, jnp.float32),
            pltpu.VMEM(field, jnp.float32),
            pltpu.VMEM((probe_count, hour_count + 2 * BAND, node_count), jnp.bfloat16),
            pltpu.VMEM((2 * hour_count, 128), jnp.bfloat16),
            pltpu.SemaphoreType.DMA((groups,)),
            pltpu.SemaphoreType.DMA,
            pltpu.SemaphoreType.DMA((TERMS, groups, 2)),
            pltpu.SemaphoreType.DMA((TERMS, groups, 2)),
            pltpu.SemaphoreType.DMA((2,)),
            pltpu.SemaphoreType.DMA((2,)),
        ],
        compiler_params=pltpu.CompilerParams(
            collective_id=0, has_side_effects=True, vmem_limit_bytes=32 * 1024 * 1024
        ),
        cost_estimate=pl.CostEstimate(
            flops=TERMS * 2 * probe_count * hour_count * node_count * NNZ * BLK,
            bytes_accessed=3 * 1024 * 1024,
            transcendentals=0,
        ),
    )(probes, lap_blocks, col_index.T, series_weights, hour_band)


def solution(mesh):
    return jax.shard_map(
        functools.partial(shards, mesh.shape["graph"], mesh.shape["tm"]),
        mesh=mesh,
        in_specs=(
            P(("groups", "rep"), "tm", "graph"),
            P(("groups", "graph"), None, None, None),
            P(("groups", "graph"), None),
            P(),
            P(None, "tm"),
        ),
        out_specs=P(("groups", "rep"), "tm", "graph"),
        check_vma=False,
    )
```

```python
import functools

import jax
import jax.numpy as jnp
from jax import lax
from jax.experimental import pallas as pl
from jax.experimental.pallas import tpu as pltpu
from jax.sharding import PartitionSpec as P

BLK = 128
NNZ = 4
BND = 4
BAND = 16
BANDW = 33
GROUP = 16
TERMS = 3


def kernel(
    graph_size,
    tm_size,
    probes,
    lap,
    col_far,
    weights_far,
    band_far,
    out,
    *scratch,
):
    probe_count, hour_count, node_count = probes.shape
    row_blocks = node_count // BLK
    group_count = hour_count // GROUP
    rows = probe_count * GROUP
    extended = scratch[: TERMS * group_count]
    (
        col,
        weights,
        hour_band,
        staged,
        lap_held,
        lap_turned,
        one,
        two,
        mixed,
        factor,
        own_sem,
        lap_sem,
        small_sem,
        send_sem,
        recv_sem,
        edge_send_sem,
        edge_recv_sem,
    ) = scratch[TERMS * group_count :]
    order = [0, group_count - 1] + list(range(1, group_count - 1))

    def ext(term, group):
        return extended[term * group_count + group]

    def hours_of(group):
        return pl.ds(group * GROUP, GROUP)

    place = lax.axis_index("graph")
    slab = lax.axis_index("tm")
    has_low, has_high = place > 0, place < graph_size - 1
    has_before, has_after = slab > 0, slab < tm_size - 1

    def own_copy(group):
        return pltpu.make_async_copy(
            probes.at[:, hours_of(group), :],
            staged.at[:, hours_of(group), :],
            own_sem.at[group],
        )

    lap_copy = pltpu.make_async_copy(lap, lap_held, lap_sem)
    small_copies = [
        pltpu.make_async_copy(source, target, small_sem.at[index])
        for index, (source, target) in enumerate(
            ((band_far, hour_band), (col_far, col), (weights_far, weights))
        )
    ]
    for group in order:
        own_copy(group).start()
    lap_copy.start()
    for copy in small_copies:
        copy.start()

    def to_high(term, group):
        return pltpu.make_async_remote_copy(
            src_ref=ext(term, group).at[pl.ds(row_blocks, BND)],
            dst_ref=ext(term, group).at[pl.ds(0, BND)],
            send_sem=send_sem.at[term, group, 0],
            recv_sem=recv_sem.at[term, group, 0],
            device_id={"graph": place + 1},
            device_id_type=pl.DeviceIdType.MESH,
        )

    def to_low(term, group):
        return pltpu.make_async_remote_copy(
            src_ref=ext(term, group).at[pl.ds(BND, BND)],
            dst_ref=ext(term, group).at[pl.ds(BND + row_blocks, BND)],
            send_sem=send_sem.at[term, group, 1],
            recv_sem=recv_sem.at[term, group, 1],
            device_id={"graph": place - 1},
            device_id_type=pl.DeviceIdType.MESH,
        )

    def to_after():
        return pltpu.make_async_remote_copy(
            src_ref=mixed.at[:, pl.ds(hour_count, BAND), :],
            dst_ref=mixed.at[:, pl.ds(0, BAND), :],
            send_sem=edge_send_sem.at[0],
            recv_sem=edge_recv_sem.at[0],
            device_id={"tm": slab + 1},
            device_id_type=pl.DeviceIdType.MESH,
        )

    def to_before():
        return pltpu.make_async_remote_copy(
            src_ref=mixed.at[:, pl.ds(BAND, BAND), :],
            dst_ref=mixed.at[:, pl.ds(BAND + hour_count, BAND), :],
            send_sem=edge_send_sem.at[1],
            recv_sem=edge_recv_sem.at[1],
            device_id={"tm": slab - 1},
            device_id_type=pl.DeviceIdType.MESH,
        )

    barrier = pltpu.get_barrier_semaphore()
    neighbours = (
        (has_low, {"graph": place - 1}),
        (has_high, {"graph": place + 1}),
        (has_before, {"tm": slab - 1}),
        (has_after, {"tm": slab + 1}),
    )
    for there, device in neighbours:

        @pl.when(there)
        def _(device=device):
            pl.semaphore_signal(
                barrier, inc=1, device_id=device, device_id_type=pl.DeviceIdType.MESH
            )

    def take_own(group):
        own_copy(group).wait()
        for block in range(row_blocks):
            ext(0, group)[BND + block] = staged[
                :, hours_of(group), pl.ds(block * BLK, BLK)
            ]

    take_own(order[0])
    peers = sum(jnp.where(there, 1, 0) for there, _ in neighbours)
    pl.semaphore_wait(barrier, peers)

    def send_both(group):
        @pl.when(has_high)
        def _():
            to_high(0, group).start()

        @pl.when(has_low)
        def _():
            to_low(0, group).start()

    depth = 2
    for index, group in enumerate(order):
        if index:
            take_own(group)
        if index < depth:
            send_both(group)

    @pl.when(jnp.logical_not(has_low))
    def _():
        for ref in extended:
            ref[pl.ds(0, BND)] = jnp.zeros((BND, probe_count, GROUP, BLK), jnp.bfloat16)

    @pl.when(jnp.logical_not(has_high))
    def _():
        for ref in extended:
            ref[pl.ds(BND + row_blocks, BND)] = jnp.zeros(
                (BND, probe_count, GROUP, BLK), jnp.bfloat16
            )

    @pl.when(jnp.logical_not(has_before))
    def _():
        mixed[:, pl.ds(0, BAND), :] = jnp.zeros((probe_count, BAND, node_count), jnp.bfloat16)

    @pl.when(jnp.logical_not(has_after))
    def _():
        mixed[:, pl.ds(BAND + hour_count, BAND), :] = jnp.zeros(
            (probe_count, BAND, node_count), jnp.bfloat16
        )

    for copy in small_copies:
        copy.wait()

    span = hour_count + 2 * BAND
    hour_in = lax.broadcasted_iota(jnp.int32, (span, hour_count), 0)
    hour_out = lax.broadcasted_iota(jnp.int32, (span, hour_count), 1)
    shift = hour_in - hour_out
    turned = jnp.zeros((span, hour_count), jnp.float32)
    for offset in range(BANDW):
        turned = jnp.where(shift == offset, hour_band[pl.ds(offset, 1), :], turned)
    turned = jnp.concatenate(
        [turned, jnp.zeros((span, 128 - hour_count), jnp.float32)], axis=1
    )
    turned = jnp.concatenate([turned, jnp.zeros((128 - span, 128), jnp.float32)], axis=0)
    whole = turned.T[:hour_count]
    high = whole.astype(jnp.bfloat16)
    low = (whole - high.astype(jnp.float32)).astype(jnp.bfloat16)
    factor[pl.ds(0, hour_count), :] = high
    factor[pl.ds(hour_count, hour_count), :] = low

    lap_copy.wait()

    def turn(row, carry):
        for entry in range(NNZ):
            lap_turned[row, pl.ds(entry * BLK, BLK), :] = lap_held[row, entry].T
        return carry

    lax.fori_loop(0, row_blocks, turn, 0)

    def lanes(block):
        return pl.ds(pl.multiple_of(block * BLK, BLK), BLK)

    def rows_of(term, group, first, count):
        source = ext(term, group)
        hours = hours_of(group)

        def body(row, carry):
            parts = [source[row + BND]]
            for entry in range(1, NNZ):
                parts.append(source[col[entry, row]])
            gathered = jnp.concatenate(
                [part.reshape(rows, BLK) for part in parts], axis=1
            )
            product = jnp.dot(
                gathered, lap_turned[row], preferred_element_type=jnp.float32
            ).reshape(probe_count, GROUP, BLK)
            here = lanes(row)
            if term == 0:
                one[:, hours, here] = product
                ext(1, group)[row + BND] = product.astype(jnp.bfloat16)
            elif term == 1:
                start = ext(0, group)[row + BND].astype(jnp.float32)
                value = 2.0 * product - start
                two[:, hours, here] = value
                ext(2, group)[row + BND] = value.astype(jnp.bfloat16)
            else:
                start = ext(0, group)[row + BND].astype(jnp.float32)
                first_term = one[:, hours, here]
                value = 2.0 * product - first_term
                mixed[:, pl.ds(BAND + group * GROUP, GROUP), here] = (
                    weights[0] * start
                    + weights[1] * first_term
                    + weights[2] * two[:, hours, here]
                    + weights[3] * value
                ).astype(jnp.bfloat16)
            return carry

        lax.fori_loop(first, first + count, body, 0, unroll=True)

    for term in range(TERMS):
        for index, group in enumerate(order):
            if term == 0 and index + depth < group_count:

                @pl.when(has_high)
                def _(group=group):
                    to_high(0, group).wait_send()

                @pl.when(has_low)
                def _(group=group):
                    to_low(0, group).wait_send()

                send_both(order[index + depth])

            @pl.when(has_low)
            def _(term=term, group=group):
                to_high(term, group).wait_recv()

            @pl.when(has_high)
            def _(term=term, group=group):
                to_low(term, group).wait_recv()

            rows_of(term, group, 0, BND)
            if term < TERMS - 1:

                @pl.when(has_low)
                def _(term=term, group=group):
                    to_low(term + 1, group).start()

            rows_of(term, group, BND, row_blocks - BND)
            if term < TERMS - 1:

                @pl.when(has_high)
                def _(term=term, group=group):
                    to_high(term + 1, group).start()

            elif group == 0:

                @pl.when(has_before)
                def _():
                    to_before().start()

            elif group == group_count - 1:

                @pl.when(has_after)
                def _():
                    to_after().start()

    @pl.when(has_before)
    def _():
        to_after().wait_recv()

    @pl.when(has_after)
    def _():
        to_before().wait_recv()

    width = 256

    def spread(index, carry):
        probe = index // (node_count // width)
        here = pl.ds(pl.multiple_of((index % (node_count // width)) * width, width), width)
        both = jnp.dot(
            factor[:, pl.ds(0, span)],
            mixed[probe, :, here],
            preferred_element_type=jnp.float32,
        )
        out[probe, :, here] = (both[:hour_count] + both[hour_count:]).astype(jnp.bfloat16)
        return carry

    lax.fori_loop(0, probe_count * (node_count // width), spread, 0, unroll=True)

    for term in range(TERMS):
        for index, group in enumerate(order):
            if term == 0 and index + depth < group_count:
                continue

            @pl.when(has_high)
            def _(term=term, group=group):
                to_high(term, group).wait_send()

            @pl.when(has_low)
            def _(term=term, group=group):
                to_low(term, group).wait_send()

    @pl.when(has_after)
    def _():
        to_after().wait_send()

    @pl.when(has_before)
    def _():
        to_before().wait_send()


def shards(graph_size, tm_size, probes, lap_blocks, col_index, series_weights, hour_band):
    probe_count, hour_count, node_count = probes.shape
    row_blocks = node_count // BLK
    groups = hour_count // GROUP
    field = (probe_count, hour_count, node_count)
    vmem = pl.BlockSpec(memory_space=pltpu.VMEM)
    far = pl.BlockSpec(memory_space=pltpu.HBM)
    return pl.pallas_call(
        functools.partial(kernel, graph_size, tm_size),
        out_shape=jax.ShapeDtypeStruct(field, jnp.bfloat16),
        in_specs=[far] * 5,
        out_specs=vmem,
        scratch_shapes=[
            pltpu.VMEM((row_blocks + 2 * BND, probe_count, GROUP, BLK), jnp.bfloat16)
            for _ in range(TERMS * groups)
        ]
        + [
            pltpu.SMEM((NNZ, row_blocks), jnp.int32),
            pltpu.SMEM(series_weights.shape, jnp.float32),
            pltpu.VMEM(hour_band.shape, jnp.float32),
            pltpu.VMEM(field, jnp.bfloat16),
            pltpu.VMEM(lap_blocks.shape, jnp.bfloat16),
            pltpu.VMEM((row_blocks, NNZ * BLK, BLK), jnp.bfloat16),
            pltpu.VMEM(field, jnp.float32),
            pltpu.VMEM(field, jnp.float32),
            pltpu.VMEM((probe_count, hour_count + 2 * BAND, node_count), jnp.bfloat16),
            pltpu.VMEM((2 * hour_count, 128), jnp.bfloat16),
            pltpu.SemaphoreType.DMA((groups,)),
            pltpu.SemaphoreType.DMA,
            pltpu.SemaphoreType.DMA((3,)),
            pltpu.SemaphoreType.DMA((TERMS, groups, 2)),
            pltpu.SemaphoreType.DMA((TERMS, groups, 2)),
            pltpu.SemaphoreType.DMA((2,)),
            pltpu.SemaphoreType.DMA((2,)),
        ],
        compiler_params=pltpu.CompilerParams(
            collective_id=0, has_side_effects=True, vmem_limit_bytes=60 * 1024 * 1024
        ),
        cost_estimate=pl.CostEstimate(
            flops=TERMS * 2 * probe_count * hour_count * node_count * NNZ * BLK,
            bytes_accessed=3 * 1024 * 1024,
            transcendentals=0,
        ),
    )(probes, lap_blocks, col_index.T, series_weights, hour_band)


def solution(mesh):
    return jax.shard_map(
        functools.partial(shards, mesh.shape["graph"], mesh.shape["tm"]),
        mesh=mesh,
        in_specs=(
            P(("groups", "rep"), "tm", "graph"),
            P(("groups", "graph"), None, None, None),
            P(("groups", "graph"), None),
            P(),
            P(None, "tm"),
        ),
        out_specs=P(("groups", "rep"), "tm", "graph"),
        check_vma=False,
    )
```

```python
import functools

import jax
import jax.numpy as jnp
from jax import lax
from jax.experimental import pallas as pl
from jax.experimental.pallas import tpu as pltpu
from jax.sharding import PartitionSpec as P

BLK = 128
NNZ = 4
BND = 4
BAND = 16
BANDW = 33
GROUP = 16
TERMS = 3


def kernel(
    graph_size,
    tm_size,
    probes,
    lap,
    col_far,
    weights_far,
    band_far,
    out,
    *scratch,
):
    probe_count, hour_count, node_count = probes.shape
    row_blocks = node_count // BLK
    group_count = hour_count // GROUP
    rows = probe_count * GROUP
    extended = scratch[: TERMS * group_count]
    (
        col,
        weights,
        hour_band,
        staged,
        lap_held,
        lap_turned,
        one,
        two,
        mixed,
        factor,
        own_sem,
        lap_sem,
        small_sem,
        send_sem,
        recv_sem,
        edge_send_sem,
        edge_recv_sem,
    ) = scratch[TERMS * group_count :]
    order = [0, group_count - 1] + list(range(1, group_count - 1))

    def ext(term, group):
        return extended[term * group_count + group]

    def hours_of(group):
        return pl.ds(group * GROUP, GROUP)

    place = lax.axis_index("graph")
    slab = lax.axis_index("tm")
    has_low, has_high = place > 0, place < graph_size - 1
    has_before, has_after = slab > 0, slab < tm_size - 1

    def own_copy(group):
        return pltpu.make_async_copy(
            probes.at[:, hours_of(group), :],
            staged.at[:, hours_of(group), :],
            own_sem.at[group],
        )

    def to_high(term, group):
        return pltpu.make_async_remote_copy(
            src_ref=ext(term, group).at[pl.ds(row_blocks, BND)],
            dst_ref=ext(term, group).at[pl.ds(0, BND)],
            send_sem=send_sem.at[term, group, 0],
            recv_sem=recv_sem.at[term, group, 0],
            device_id={"graph": place + 1},
            device_id_type=pl.DeviceIdType.MESH,
        )

    def to_low(term, group):
        return pltpu.make_async_remote_copy(
            src_ref=ext(term, group).at[pl.ds(BND, BND)],
            dst_ref=ext(term, group).at[pl.ds(BND + row_blocks, BND)],
            send_sem=send_sem.at[term, group, 1],
            recv_sem=recv_sem.at[term, group, 1],
            device_id={"graph": place - 1},
            device_id_type=pl.DeviceIdType.MESH,
        )

    def to_after():
        return pltpu.make_async_remote_copy(
            src_ref=mixed.at[:, pl.ds(hour_count, BAND), :],
            dst_ref=mixed.at[:, pl.ds(0, BAND), :],
            send_sem=edge_send_sem.at[0],
            recv_sem=edge_recv_sem.at[0],
            device_id={"tm": slab + 1},
            device_id_type=pl.DeviceIdType.MESH,
        )

    def to_before():
        return pltpu.make_async_remote_copy(
            src_ref=mixed.at[:, pl.ds(BAND, BAND), :],
            dst_ref=mixed.at[:, pl.ds(BAND + hour_count, BAND), :],
            send_sem=edge_send_sem.at[1],
            recv_sem=edge_recv_sem.at[1],
            device_id={"tm": slab - 1},
            device_id_type=pl.DeviceIdType.MESH,
        )

    barrier = pltpu.get_barrier_semaphore()
    neighbours = (
        (has_low, {"graph": place - 1}),
        (has_high, {"graph": place + 1}),
        (has_before, {"tm": slab - 1}),
        (has_after, {"tm": slab + 1}),
    )
    for there, device in neighbours:

        @pl.when(there)
        def _(device=device):
            pl.semaphore_signal(
                barrier, inc=1, device_id=device, device_id_type=pl.DeviceIdType.MESH
            )

    lap_copy = pltpu.make_async_copy(lap, lap_held, lap_sem)
    small_copies = [
        pltpu.make_async_copy(source, target, small_sem.at[index])
        for index, (source, target) in enumerate(
            ((band_far, hour_band), (col_far, col), (weights_far, weights))
        )
    ]
    for group in order:
        own_copy(group).start()
    lap_copy.start()
    for copy in small_copies:
        copy.start()

    def take_own(group):
        own_copy(group).wait()
        for block in range(row_blocks):
            ext(0, group)[BND + block] = staged[
                :, hours_of(group), pl.ds(block * BLK, BLK)
            ]

    take_own(order[0])
    peers = sum(jnp.where(there, 1, 0) for there, _ in neighbours)
    pl.semaphore_wait(barrier, peers)

    def send_both(group):
        @pl.when(has_high)
        def _():
            to_high(0, group).start()

        @pl.when(has_low)
        def _():
            to_low(0, group).start()

    depth = 4
    for index, group in enumerate(order):
        if index:
            take_own(group)
        if index < depth:
            send_both(group)

    @pl.when(jnp.logical_not(has_low))
    def _():
        for ref in extended:
            ref[pl.ds(0, BND)] = jnp.zeros((BND, probe_count, GROUP, BLK), jnp.bfloat16)

    @pl.when(jnp.logical_not(has_high))
    def _():
        for ref in extended:
            ref[pl.ds(BND + row_blocks, BND)] = jnp.zeros(
                (BND, probe_count, GROUP, BLK), jnp.bfloat16
            )

    @pl.when(jnp.logical_not(has_before))
    def _():
        mixed[:, pl.ds(0, BAND), :] = jnp.zeros((probe_count, BAND, node_count), jnp.bfloat16)

    @pl.when(jnp.logical_not(has_after))
    def _():
        mixed[:, pl.ds(BAND + hour_count, BAND), :] = jnp.zeros(
            (probe_count, BAND, node_count), jnp.bfloat16
        )

    for copy in small_copies:
        copy.wait()

    span = hour_count + 2 * BAND
    hour_in = lax.broadcasted_iota(jnp.int32, (span, hour_count), 0)
    hour_out = lax.broadcasted_iota(jnp.int32, (span, hour_count), 1)
    shift = hour_in - hour_out
    turned = jnp.zeros((span, hour_count), jnp.float32)
    for offset in range(BANDW):
        turned = jnp.where(shift == offset, hour_band[pl.ds(offset, 1), :], turned)
    turned = jnp.concatenate(
        [turned, jnp.zeros((span, 128 - hour_count), jnp.float32)], axis=1
    )
    turned = jnp.concatenate([turned, jnp.zeros((128 - span, 128), jnp.float32)], axis=0)
    whole = turned.T[:hour_count]
    high = whole.astype(jnp.bfloat16)
    low = (whole - high.astype(jnp.float32)).astype(jnp.bfloat16)
    factor[pl.ds(0, hour_count), :] = high
    factor[pl.ds(hour_count, hour_count), :] = low

    lap_copy.wait()

    def turn(row, carry):
        for entry in range(NNZ):
            lap_turned[row, pl.ds(entry * BLK, BLK), :] = lap_held[row, entry].T
        return carry

    lax.fori_loop(0, row_blocks, turn, 0)

    def lanes(block):
        return pl.ds(pl.multiple_of(block * BLK, BLK), BLK)

    def rows_of(term, group, first, count):
        source = ext(term, group)
        hours = hours_of(group)

        def body(row, carry):
            parts = [source[row + BND]]
            for entry in range(1, NNZ):
                parts.append(source[col[entry, row]])
            gathered = jnp.concatenate(
                [part.reshape(rows, BLK) for part in parts], axis=1
            )
            product = jnp.dot(
                gathered, lap_turned[row], preferred_element_type=jnp.float32
            ).reshape(probe_count, GROUP, BLK)
            here = lanes(row)
            if term == 0:
                one[:, hours, here] = product
                ext(1, group)[row + BND] = product.astype(jnp.bfloat16)
            elif term == 1:
                start = ext(0, group)[row + BND].astype(jnp.float32)
                value = 2.0 * product - start
                two[:, hours, here] = value
                ext(2, group)[row + BND] = value.astype(jnp.bfloat16)
            else:
                start = ext(0, group)[row + BND].astype(jnp.float32)
                first_term = one[:, hours, here]
                value = 2.0 * product - first_term
                mixed[:, pl.ds(BAND + group * GROUP, GROUP), here] = (
                    weights[0] * start
                    + weights[1] * first_term
                    + weights[2] * two[:, hours, here]
                    + weights[3] * value
                ).astype(jnp.bfloat16)
            return carry

        lax.fori_loop(first, first + count, body, 0, unroll=True)

    for term in range(TERMS):
        for index, group in enumerate(order):
            if term == 0 and index + depth < group_count:

                @pl.when(has_high)
                def _(group=group):
                    to_high(0, group).wait_send()

                @pl.when(has_low)
                def _(group=group):
                    to_low(0, group).wait_send()

                send_both(order[index + depth])

            @pl.when(has_low)
            def _(term=term, group=group):
                to_high(term, group).wait_recv()

            @pl.when(has_high)
            def _(term=term, group=group):
                to_low(term, group).wait_recv()

            rows_of(term, group, 0, BND)
            if term < TERMS - 1:

                @pl.when(has_low)
                def _(term=term, group=group):
                    to_low(term + 1, group).start()

            rows_of(term, group, BND, row_blocks - BND)
            if term < TERMS - 1:

                @pl.when(has_high)
                def _(term=term, group=group):
                    to_high(term + 1, group).start()

            elif group == 0:

                @pl.when(has_before)
                def _():
                    to_before().start()

            elif group == group_count - 1:

                @pl.when(has_after)
                def _():
                    to_after().start()

    @pl.when(has_before)
    def _():
        to_after().wait_recv()

    @pl.when(has_after)
    def _():
        to_before().wait_recv()

    width = 256

    def spread(index, carry):
        probe = index // (node_count // width)
        here = pl.ds(pl.multiple_of((index % (node_count // width)) * width, width), width)
        both = jnp.dot(
            factor[:, pl.ds(0, span)],
            mixed[probe, :, here],
            preferred_element_type=jnp.float32,
        )
        out[probe, :, here] = (both[:hour_count] + both[hour_count:]).astype(jnp.bfloat16)
        return carry

    lax.fori_loop(0, probe_count * (node_count // width), spread, 0, unroll=True)

    for term in range(TERMS):
        for index, group in enumerate(order):
            if term == 0 and index + depth < group_count:
                continue

            @pl.when(has_high)
            def _(term=term, group=group):
                to_high(term, group).wait_send()

            @pl.when(has_low)
            def _(term=term, group=group):
                to_low(term, group).wait_send()

    @pl.when(has_after)
    def _():
        to_after().wait_send()

    @pl.when(has_before)
    def _():
        to_before().wait_send()


def shards(graph_size, tm_size, probes, lap_blocks, col_index, series_weights, hour_band):
    probe_count, hour_count, node_count = probes.shape
    row_blocks = node_count // BLK
    groups = hour_count // GROUP
    field = (probe_count, hour_count, node_count)
    vmem = pl.BlockSpec(memory_space=pltpu.VMEM)
    far = pl.BlockSpec(memory_space=pltpu.HBM)
    return pl.pallas_call(
        functools.partial(kernel, graph_size, tm_size),
        out_shape=pltpu.VMEM(field, jnp.bfloat16),
        in_specs=[far] * 5,
        out_specs=vmem,
        scratch_shapes=[
            pltpu.VMEM((row_blocks + 2 * BND, probe_count, GROUP, BLK), jnp.bfloat16)
            for _ in range(TERMS * groups)
        ]
        + [
            pltpu.SMEM((NNZ, row_blocks), jnp.int32),
            pltpu.SMEM(series_weights.shape, jnp.float32),
            pltpu.VMEM(hour_band.shape, jnp.float32),
            pltpu.VMEM(field, jnp.bfloat16),
            pltpu.VMEM(lap_blocks.shape, jnp.bfloat16),
            pltpu.VMEM((row_blocks, NNZ * BLK, BLK), jnp.bfloat16),
            pltpu.VMEM(field, jnp.float32),
            pltpu.VMEM(field, jnp.float32),
            pltpu.VMEM((probe_count, hour_count + 2 * BAND, node_count), jnp.bfloat16),
            pltpu.VMEM((2 * hour_count, 128), jnp.bfloat16),
            pltpu.SemaphoreType.DMA((groups,)),
            pltpu.SemaphoreType.DMA,
            pltpu.SemaphoreType.DMA((3,)),
            pltpu.SemaphoreType.DMA((TERMS, groups, 2)),
            pltpu.SemaphoreType.DMA((TERMS, groups, 2)),
            pltpu.SemaphoreType.DMA((2,)),
            pltpu.SemaphoreType.DMA((2,)),
        ],
        compiler_params=pltpu.CompilerParams(
            collective_id=0, has_side_effects=True, vmem_limit_bytes=60 * 1024 * 1024
        ),
        cost_estimate=pl.CostEstimate(
            flops=TERMS * 2 * probe_count * hour_count * node_count * NNZ * BLK,
            bytes_accessed=3 * 1024 * 1024,
            transcendentals=0,
        ),
    )(probes, lap_blocks, col_index.T, series_weights, hour_band)


def solution(mesh):
    return jax.shard_map(
        functools.partial(shards, mesh.shape["graph"], mesh.shape["tm"]),
        mesh=mesh,
        in_specs=(
            P(("groups", "rep"), "tm", "graph"),
            P(("groups", "graph"), None, None, None),
            P(("groups", "graph"), None),
            P(),
            P(None, "tm"),
        ),
        out_specs=P(("groups", "rep"), "tm", "graph"),
        check_vma=False,
    )
```
